256 devices in a mesh: rep: 8 (over z_lo, core), fsdp: 32 (over x, z_hi, y).
Axes of the slice: x: 4, y: 4, z: 8 (z_hi: 2, z_lo: 4; z = z_hi * 4 + z_lo), core: 2. Of those that a mesh axis runs over, the one named last changes fastest.
Arguments:
- activations: bfloat16 [131072, 5120], P(('rep', 'fsdp')), may hold values from -6 to 6
- cotangents: bfloat16 [131072, 1024], P(('rep', 'fsdp')), may hold values from -0.01171875 to 0.01171875
- weights: bfloat16 [5120, 1024], P('fsdp'), may hold values from -0.078125 to 0.078125
- momentum: float32 [8, 5120, 1024], P('rep', 'fsdp'), may hold values from -6 to 6
- positions: int32 [8, 5120, 16, 8], P('rep', 'fsdp'), may hold values from 0 to 63, as said below
Outputs:
- new_momentum: float32 [8, 5120, 1024], P('rep', 'fsdp')
- new_weights: bfloat16 [5120, 1024], P('fsdp')
- new_keys: bfloat16 [131072, 1024], P(('rep', 'fsdp'))
The draws below stay inside these ranges and needn't reach their ends.
Inputs may be any that keep to these rules, and one draw needn't show every extreme that they name: The 8 positions of one span are distinct.
All inputs are finite; a program needn't handle non-finite values.
Results may differ from the reference program's by a relative error of at most 0.01.
Values may be sent and summed in bfloat16 or wider, within the bound.
A program may use at most 128 MiB of HBM per device.

```python
import math
import jax
import jax.numpy as jnp
from jax import lax

D = 5120
KV = 1024
TOK_DEV = 512
TOKENS = 131072
N_REP = 8
N_FSDP = 32


def draw_positions(key, part):
    key = jax.random.fold_in(key, 11)
    scores = jax.random.randint(key, (N_REP, D, KV // 64, 64), 0, 1 << 20, dtype=jnp.int32)
    scores = scores * 64 + jnp.arange(64, dtype=jnp.int32)
    unused, picked = lax.top_k(scores, 8)
    return picked.astype(jnp.int32)


def shard_levels(key, dims, shards, least, high):
    loudness = 1.0
    for axis_at, blocks in shards:
        draws = jax.random.uniform(jax.random.fold_in(jax.random.fold_in(key, 6), axis_at), (blocks,), jnp.float32, least / len(shards), high / len(shards))
        loudness = loudness * jnp.repeat(jnp.exp(draws), dims[axis_at] // blocks).reshape((-1,) + (1,) * (len(dims) - 1 - axis_at))
    return loudness


def centred(rng, extent, deviation, bound, cuts=(), kind=jnp.bfloat16):
    entries = deviation * jax.random.normal(rng, extent, jnp.float32)
    if cuts:
        entries = entries * shard_levels(rng, extent, cuts, -0.22, 0.18)
    return jnp.clip(entries, -bound, bound).astype(kind)


def setup_inputs(seed: int = 0) -> dict:
    key_of = jax.random.split(jax.random.key(seed), 6)
    return {
        "activations": centred(key_of[0], (TOKENS, D), 1.0, 6.0, ((0, 256),)),
        "cotangents": centred(key_of[1], (TOKENS, KV), (0.25 * (TOK_DEV * N_FSDP) ** -0.5), 0.01171875, ((0, 256),)),
        "weights": centred(key_of[2], (D, KV), D ** -0.5, 0.078125, ((0, 32),)),
        "momentum": centred(key_of[3], (N_REP, D, KV), 1.0, 6.0, ((0, 8), (1, 32)), jnp.float32),
        "positions": draw_positions(jax.random.fold_in(key_of[5], 71), 0),
    }


def dct_table():
    freq = jnp.arange(64, dtype=jnp.float32)[:, None]
    place = jnp.arange(64, dtype=jnp.float32)[None, :]
    weight = jnp.where(freq == 0, math.sqrt(1.0 / 64), math.sqrt(2.0 / 64))
    return weight * jnp.cos(math.pi * (2.0 * place + 1.0) * freq / 128.0)

def reference(activations, cotangents, weights, momentum, positions):
    table = dct_table()
    group_tokens = TOK_DEV * N_FSDP
    slots = jnp.arange(64, dtype=jnp.int32)

    def one_group(index):
        acts = lax.dynamic_slice_in_dim(activations, (index * group_tokens).astype(jnp.int32), group_tokens, 0)
        cots = lax.dynamic_slice_in_dim(cotangents, (index * group_tokens).astype(jnp.int32), group_tokens, 0)
        acts = acts.reshape(N_FSDP, TOK_DEV, D)
        cots = cots.reshape(N_FSDP, TOK_DEV, KV)

        def add_block(total, block):
            term = lax.dot_general(block[0], block[1], (((0,), (0,)), ((), ())), preferred_element_type=jnp.float32)
            term = lax.optimization_barrier(term.astype(jnp.bfloat16))
            return (total + term.astype(jnp.float32), None)
        grad, unused = lax.scan(add_block, jnp.zeros((D, KV), jnp.float32), (acts, cots))
        moment = 0.9 * momentum[index] + grad
        spans = moment.reshape(D, KV // 64, 64)
        coeffs = jnp.einsum('ijn,kn->ijk', spans, table, precision=lax.Precision.HIGHEST)
        pos = positions[index]
        kept = jnp.take_along_axis(coeffs, pos, axis=2)
        onehot = (pos[..., None] == slots).astype(jnp.float32)
        sparse = lax.optimization_barrier(jnp.sum(kept[..., None] * onehot, axis=2))
        sent = jnp.einsum('ijk,kn->ijn', sparse, table, precision=lax.Precision.HIGHEST)
        return (moment - sent.reshape(D, KV), sparse)
    new_momentum, sparse_all = lax.map(one_group, jnp.arange(N_REP, dtype=jnp.int32))
    total = lax.optimization_barrier(jnp.sum(sparse_all, axis=0))
    update = jnp.einsum('ijk,kn->ijn', total, table, precision=lax.Precision.HIGHEST).reshape(D, KV) / N_REP
    new_weights = (weights.astype(jnp.float32) - 0.03 * update).astype(jnp.bfloat16)
    new_keys = jnp.dot(activations, new_weights, preferred_element_type=jnp.float32).astype(jnp.bfloat16)
    return (new_momentum, new_weights, new_keys)
```

```python
import functools
import math

import jax
import jax.numpy as jnp
import numpy as np
from jax import lax
from jax.experimental import pallas as pl
from jax.experimental.pallas import tpu as pltpu
from jax.sharding import PartitionSpec as P

MESH = pl.DeviceIdType.MESH
BF = jnp.bfloat16
F32 = jnp.float32
N_COPIES = 128


def transforms():
    k = np.arange(64, dtype=np.float64)[:, None]
    n = np.arange(64, dtype=np.float64)[None, :]
    table = np.where(k == 0, math.sqrt(1.0 / 64), math.sqrt(2.0 / 64)) * np.cos(math.pi * (2 * n + 1) * k / 128)
    back = np.kron(np.eye(4), table).astype(np.float32)
    high = back.astype(jnp.bfloat16)
    low = (back - high.astype(np.float32)).astype(jnp.bfloat16)
    return np.stack([high.T, low.T, high, low])


def dot3(value, high, low):
    top = value.astype(BF)
    rest = (value - top.astype(F32)).astype(BF)
    dot = functools.partial(jnp.dot, preferred_element_type=F32)
    return dot(top, high) + (dot(rest, high) + dot(top, low))


def kernel(
    acts, cots, weights, momentum, pos, dct,
    new_mom, new_w, keys,
    sib_acts, part, hop, plus, minus, hop2, plus2, minus2, cross, cross_in,
    mask, sent, sib_in, pair, pair_in, gathered, total, far_keys,
    send_sems, recv_sems,
):
    rep, fsdp = lax.axis_index("rep"), lax.axis_index("fsdp")
    x, zh, y = fsdp // 8, (fsdp // 4) % 2, fsdp % 4
    zl, core = rep // 2, rep % 2
    z = zh * 4 + zl
    me = (x, y)

    def device(dx=0, dy=0, dz=0, flip=False):
        nz = (z + dz) % 8
        return (
            (nz % 4) * 2 + ((1 - core) if flip else core),
            ((x + dx) % 4) * 8 + (nz // 4) * 4 + (y + dy) % 4,
        )

    def along(axis, step):
        return device(dx=step) if axis == 0 else device(dy=step)

    used = [0]

    def send(src, dst, target):
        slot = used[0]
        used[0] += 1
        copy = pltpu.make_async_remote_copy(
            src_ref=src, dst_ref=dst, send_sem=send_sems.at[slot], recv_sem=recv_sems.at[slot],
            device_id=target, device_id_type=MESH,
        )
        copy.start()
        return copy

    sent_copies = []

    def push(src, dst, target):
        copy = send(src, dst, target)
        sent_copies.append(copy)
        return copy

    peers = [along(0, 1), along(0, -1), along(1, 1), along(1, -1), device(flip=True)]
    peers += [device(dz=d) for d in range(1, 8)]
    barrier = pltpu.get_barrier_semaphore()
    for peer in peers:
        pl.semaphore_signal(barrier, inc=1, device_id=peer, device_id_type=MESH)
    pl.semaphore_wait(barrier, len(peers))

    def multiply(half, ux):
        unit = ux * 2 + half
        columns = acts[:, pl.ds(pl.multiple_of(unit * 640, 128), 640)]
        out = lax.dot_general(columns, cots[...], (((0,), (0,)), ((), ())), preferred_element_type=F32).astype(BF)
        for uy in range(4):
            part[0, half, ux, uy] = out[uy * 160 : uy * 160 + 80]
            part[1, half, uy, ux] = out[uy * 160 + 80 : uy * 160 + 160]

    def chunk(s, half, j, h):
        return part.at[s, half, j, pl.ds(2 * h, 2)]

    class First:
        def __init__(self, s, turn, half):
            self.s, self.turn, self.half, self.p = s, turn, half, me[s]

        def open(self):
            s, turn, half, p = self.s, self.turn, self.half, self.p
            across = (p + 2) % 4
            self.up1 = push(chunk(s, half, across, 0), hop.at[s, turn, 0], along(s, 1))
            self.down1 = push(chunk(s, half, across, 1), hop.at[s, turn, 1], along(s, -1))

        def open2(self):
            s, turn, half, p = self.s, self.turn, self.half, self.p
            after, before = (p + 1) % 4, (p + 3) % 4
            self.up2 = push(chunk(s, half, after, 1), plus.at[s, turn, pl.ds(2, 2)], along(s, 1))
            self.down2 = push(chunk(s, half, before, 0), minus.at[s, turn, pl.ds(0, 2)], along(s, -1))

        def relay(self):
            s, turn, half, p = self.s, self.turn, self.half, self.p
            after, before = (p + 1) % 4, (p + 3) % 4
            self.up1.wait_recv()
            ref = chunk(s, half, after, 0)
            ref[...] = (ref[...].astype(F32) + hop[s, turn, 0].astype(F32)).astype(BF)
            self.up3 = push(ref, plus.at[s, turn, pl.ds(0, 2)], along(s, 1))
            self.down1.wait_recv()
            ref = chunk(s, half, before, 1)
            ref[...] = (ref[...].astype(F32) + hop[s, turn, 1].astype(F32)).astype(BF)
            self.down3 = push(ref, minus.at[s, turn, pl.ds(2, 2)], along(s, -1))

        def close(self):
            s, turn, half, p = self.s, self.turn, self.half, self.p
            for copy in (self.up2, self.down2, self.up3, self.down3):
                copy.wait_recv()
            ref = part.at[s, half, p]
            ref[...] = (
                ref[...].astype(F32) + plus[s, turn].astype(F32) + minus[s, turn].astype(F32)
            ).astype(BF)

    class Second:
        def __init__(self, s, turn, half):
            self.s, self.turn, self.half, self.p1, self.p = s, turn, half, me[s], me[1 - s]

        def block(self, j, h):
            return part.at[self.s, self.half, self.p1, j, :, pl.ds(512 * h, 512)]

        def open(self):
            s, turn, p = self.s, self.turn, self.p
            across, after, before = (p + 2) % 4, (p + 1) % 4, (p + 3) % 4
            ax = 1 - s
            self.up1 = push(self.block(across, 0), hop2.at[s, turn, 0], along(ax, 1))
            self.down1 = push(self.block(across, 1), hop2.at[s, turn, 1], along(ax, -1))
            self.up2 = push(self.block(after, 1), plus2.at[s, turn, 1], along(ax, 1))
            self.down2 = push(self.block(before, 0), minus2.at[s, turn, 0], along(ax, -1))

        def relay(self):
            s, turn, p = self.s, self.turn, self.p
            after, before = (p + 1) % 4, (p + 3) % 4
            ax = 1 - s
            self.up1.wait_recv()
            ref = self.block(after, 0)
            ref[...] = (ref[...].astype(F32) + hop2[s, turn, 0].astype(F32)).astype(BF)
            self.up3 = push(ref, plus2.at[s, turn, 0], along(ax, 1))
            self.down1.wait_recv()
            ref = self.block(before, 1)
            ref[...] = (ref[...].astype(F32) + hop2[s, turn, 1].astype(F32)).astype(BF)
            self.down3 = push(ref, minus2.at[s, turn, 1], along(ax, -1))

        def arrive(self):
            for copy in (self.up2, self.down2, self.up3, self.down3):
                copy.wait_recv()

        def value(self, g):
            s, turn = self.s, self.turn
            h, lanes = g // 2, slice(g % 2 * 256, g % 2 * 256 + 256)
            return (
                part[s, self.half, self.p1, self.p, :, g * 256 : g * 256 + 256].astype(F32)
                + plus2[s, turn, h, :, lanes].astype(F32)
                + minus2[s, turn, h, :, lanes].astype(F32)
            )

    other = 1 - zh
    firsts = [[First(s, 0, other), First(s, 1, zh)] for s in range(2)]
    seconds = [[Second(s, 0, other), Second(s, 1, zh)] for s in range(2)]

    multiply(other, (x + 2) % 4)
    firsts[0][0].open()
    multiply(other, (x + 1) % 4)
    multiply(other, (x + 3) % 4)
    firsts[0][0].open2()
    multiply(other, x)
    firsts[1][0].open()
    firsts[1][0].open2()
    pl.loop(0, 4)(lambda k: multiply(zh, (x + 2 + k) % 4))

    firsts[0][0].relay()
    firsts[0][1].open()
    firsts[0][1].open2()
    firsts[1][0].relay()
    firsts[1][1].open()
    firsts[1][1].open2()

    acts_copy = push(acts, sib_acts, device(flip=True))
    places = pos[...].astype(F32).astype(BF)
    lane = lax.broadcasted_iota(jnp.int32, (128, 1024), 1)
    row = lax.broadcasted_iota(jnp.int32, (128, 1024), 0)
    slot = (lax.broadcasted_iota(jnp.int32, (160, 1024), 1) % 64).astype(F32)
    mask[...] = jnp.zeros_like(mask)
    for t in range(8):
        pick = (row == lane // 64 * 8 + t).astype(F32).astype(BF)
        at = lax.dot_general(places, pick, (((0,), (0,)), ((), ())), preferred_element_type=F32)
        mask[...] += (at == slot).astype(F32)

    firsts[0][0].close()
    seconds[0][0].open()
    firsts[1][0].close()
    seconds[1][0].open()
    seconds[0][0].relay()
    firsts[0][1].relay()
    seconds[1][0].relay()
    firsts[1][1].relay()

    crossing = []
    for s in range(2):
        seconds[s][0].arrive()
        for g in range(4):
            cross[s, :, g * 256 : g * 256 + 256] = seconds[s][0].value(g).astype(BF)
        crossing.append(push(cross.at[s], cross_in.at[s], device(dz=4)))

    for s in range(2):
        firsts[s][1].close()
        seconds[s][1].open()
    for s in range(2):
        seconds[s][1].relay()

    sib_copies = []
    for s in range(2):
        seconds[s][1].arrive()
        crossing[s].wait_recv()
        rows = slice(s * 80, s * 80 + 80)
        for g in range(4):
            cols = slice(g * 256, g * 256 + 256)
            grad = seconds[s][1].value(g) + cross_in[s, :, cols].astype(F32)
            moment = 0.9 * momentum[rows, cols] + grad
            sparse = dot3(moment, dct[0], dct[1]) * mask[rows, cols]
            decoded = dot3(sparse, dct[2], dct[3])
            new_mom[rows, cols] = moment - decoded
            decoded = decoded.astype(BF)
            sent[s, 2 * g] = decoded[:, :128]
            sent[s, 2 * g + 1] = decoded[:, 128:]
        sib_copies.append(push(sent.at[s, pl.ds(4 * (1 - core), 4)], sib_in.at[s], device(flip=True)))

    pair_copies = []
    for s in range(2):
        sib_copies[s].wait_recv()
        for k in range(4):
            pair[s, k] = (sent[s, 4 * core + k].astype(F32) + sib_in[s, k].astype(F32)).astype(BF)
        copies = []
        for d in range(1, 4):
            peer = (zl + d) % 4
            copies.append(push(pair.at[s, peer], pair_in.at[s, d - 1], (peer * 2 + core, fsdp)))
        pair_copies.append(copies)

    own = 2 * x + zh
    q_me, lanes_me = zl // 2, pl.ds(pl.multiple_of((zl % 2) * 128, 128), 128)
    spread = []
    for s in range(2):
        for copy in pair_copies[s]:
            copy.wait_recv()
        update = pair[s, zl].astype(F32)
        for d in range(3):
            update = update + pair_in[s, d].astype(F32)
        old = weights[s * 80 : s * 80 + 80, pl.ds(pl.multiple_of((core * 4 + zl) * 128, 128), 128)]
        gathered[q_me, own, y, s, :, lanes_me] = (old.astype(F32) - (0.03 / 8) * update).astype(BF)
        block = gathered.at[q_me, own, y, s, :, lanes_me]
        spread.append([push(block, block, device(dz=d)) for d in range(1, 8)])

    near = []
    for s in range(2):
        for copy in spread[s]:
            copy.wait_recv()
        block = gathered.at[:, pl.ds(2 * x, 2), y, s]
        near.append([push(block, block, along(s, 1)), push(block, block, along(s, -1))])
        for q in range(2):
            lanes = pl.ds(pl.multiple_of(core * 512 + q * 256, 256), 256)
            new_w[s * 80 : s * 80 + 80, lanes] = gathered[q, own, y, s]
            mine = gathered.at[q, own, y, s]
            near[s].append(push(mine, new_w.at[pl.ds(s * 80, 80), lanes], device(flip=True)))

    for s in range(2):
        up, down = near[s][:2]
        up.wait_recv()
        down.wait_recv()
        spots = []
        for h, step in ((0, -1), (1, 1)):
            if s == 0:
                spots.append(gathered.at[:, 2 * ((x + step) % 4) + h, y, s])
            else:
                spots.append(gathered.at[:, 2 * x + h, (y + step) % 4, s])
        near[s].append(push(spots[0], spots[0], along(s, 1)))
        near[s].append(push(spots[1], spots[1], along(s, -1)))

    far = [[None, None], [None, None]]
    for s in range(2):
        for copy in near[s][4:]:
            copy.wait_recv()
        for q in range(2):
            if s == 0:
                block = gathered.at[q, :, y, s]
            else:
                block = gathered.at[q, pl.ds(2 * x, 2), :, s]
            far[s][q] = [push(block, block, along(1 - s, 1)), push(block, block, along(1 - s, -1))]
    for q in range(2):
        for s in range(2):
            for copy in far[s][q]:
                copy.wait_recv()
            spots = []
            for h, step in ((0, -1), (1, 1)):
                if s == 0:
                    spots.append(gathered.at[q, pl.ds(4 * h, 4), (y + step) % 4, s])
                else:
                    spots.append(gathered.at[q, 2 * ((x + step) % 4) + h, :, s])
            far[s][q] = [
                push(spots[0], spots[0], along(1 - s, 1)),
                push(spots[1], spots[1], along(1 - s, -1)),
            ]

    acts_copy.wait_recv()
    back = []
    for q in range(2):
        for s in range(2):
            for copy in far[s][q]:
                copy.wait_recv()
        total[...] = jnp.zeros_like(total)

        @pl.loop(0, 4)
        def _(k):
            rows = gathered[q, pl.ds(2 * k, 2)].reshape(1280, 256)
            lanes = pl.ds(pl.multiple_of(k * 1280, 128), 1280)
            total[0] += jnp.dot(sib_acts[:, lanes], rows, preferred_element_type=F32)
            total[1] += jnp.dot(acts[:, lanes], rows, preferred_element_type=F32)

        lanes = pl.ds(pl.multiple_of(core * 512 + q * 256, 256), 256)
        far_keys[q] = total[0].astype(BF)
        back.append(push(far_keys.at[q], keys.at[:, lanes], device(flip=True)))
        keys[:, lanes] = total[1].astype(BF)

    for copy in near[0][2:4] + near[1][2:4] + back:
        copy.wait_recv()
    for copy in sent_copies:
        copy.wait_send()


def on_device(activations, cotangents, weights, momentum, positions):
    vmem = pl.BlockSpec(memory_space=pltpu.VMEM)
    pos = positions[0].transpose(1, 2, 0).reshape(128, 160)
    dma = pltpu.SemaphoreType.DMA((N_COPIES,))
    new_mom, new_w, keys = pl.pallas_call(
        kernel,
        name="step",
        out_shape=(
            jax.ShapeDtypeStruct((160, 1024), F32),
            jax.ShapeDtypeStruct((160, 1024), BF),
            jax.ShapeDtypeStruct((512, 1024), BF),
        ),
        in_specs=[vmem] * 6,
        out_specs=(vmem, vmem, vmem),
        scratch_shapes=[
            pltpu.VMEM((512, 5120), BF),
            pltpu.VMEM((2, 2, 4, 4, 80, 1024), BF),
            pltpu.VMEM((2, 2, 2, 2, 80, 1024), BF),
            pltpu.VMEM((2, 2, 4, 80, 1024), BF),
            pltpu.VMEM((2, 2, 4, 80, 1024), BF),
            pltpu.VMEM((2, 2, 2, 80, 512), BF),
            pltpu.VMEM((2, 2, 2, 80, 512), BF),
            pltpu.VMEM((2, 2, 2, 80, 512), BF),
            pltpu.VMEM((2, 80, 1024), BF),
            pltpu.VMEM((2, 80, 1024), BF),
            pltpu.VMEM((160, 1024), F32),
            pltpu.VMEM((2, 8, 80, 128), BF),
            pltpu.VMEM((2, 4, 80, 128), BF),
            pltpu.VMEM((2, 4, 80, 128), BF),
            pltpu.VMEM((2, 3, 80, 128), BF),
            pltpu.VMEM((2, 8, 4, 2, 80, 256), BF),
            pltpu.VMEM((2, 512, 256), F32),
            pltpu.VMEM((2, 512, 256), BF),
            dma,
            dma,
        ],
        compiler_params=pltpu.CompilerParams(
            collective_id=0, has_side_effects=True, vmem_limit_bytes=60 * 2**20
        ),
    )(activations, cotangents, weights, momentum[0], pos, jnp.asarray(transforms()))
    return new_mom[None], new_w, keys


def solution(mesh):
    placed = (
        P(("rep", "fsdp"), None),
        P(("rep", "fsdp"), None),
        P("fsdp", None),
        P("rep", "fsdp", None),
        P("rep", "fsdp", None, None),
    )
    return jax.shard_map(
        on_device,
        mesh=mesh,
        in_specs=placed,
        out_specs=(P("rep", "fsdp", None), P("fsdp", None), P(("rep", "fsdp"), None)),
        check_vma=False,
    )
```

```python
import functools
import math

import jax
import jax.numpy as jnp
import numpy as np
from jax import lax
from jax.experimental import pallas as pl
from jax.experimental.pallas import tpu as pltpu
from jax.sharding import PartitionSpec as P

MESH = pl.DeviceIdType.MESH
BF = jnp.bfloat16
F32 = jnp.float32
N_COPIES = 192
WIDE = 512


def transforms():
    k = np.arange(64, dtype=np.float64)[:, None]
    n = np.arange(64, dtype=np.float64)[None, :]
    table = np.where(k == 0, math.sqrt(1.0 / 64), math.sqrt(2.0 / 64)) * np.cos(math.pi * (2 * n + 1) * k / 128)
    back = np.kron(np.eye(4), table).astype(np.float32)
    high = back.astype(jnp.bfloat16)
    low = (back - high.astype(np.float32)).astype(jnp.bfloat16)
    return np.stack([high.T, low.T, high, low])


def dot3(value, high, low):
    top = value.astype(BF)
    rest = (value - top.astype(F32)).astype(BF)
    dot = functools.partial(jnp.dot, preferred_element_type=F32)
    return dot(top, high) + (dot(rest, high) + dot(top, low))


def kernel(
    acts_in, cots_in, weights_in, momentum_in, pos_in, dct_in,
    new_mom, new_w, keys,
    acts, cots, weights, momentum, pos, dct,
    sib_acts, part, hop, plus, minus, hop2, plus2, minus2, cross, cross_in,
    mask, sent, sib_in, pair, pair_in, gathered, total, far_keys,
    load_sems, send_sems, recv_sems,
):
    rep, fsdp = lax.axis_index("rep"), lax.axis_index("fsdp")
    x, zh, y = fsdp // 8, (fsdp // 4) % 2, fsdp % 4
    zl, core = rep // 2, rep % 2
    z = zh * 4 + zl
    other = 1 - zh

    def device(dx=0, dy=0, dz=0, flip=False):
        nz = (z + 8 + dz) % 8
        return (
            (nz % 4) * 2 + ((1 - core) if flip else core),
            ((x + 4 + dx) % 4) * 8 + (nz // 4) * 4 + (y + 4 + dy) % 4,
        )

    def along(axis, step):
        return device(dx=step) if axis == 0 else device(dy=step)

    peers = [along(axis, step) for axis in range(2) for step in (1, 2, 3)]
    peers += [device(dz=d) for d in range(1, 8)] + [device(flip=True)]
    barrier = pltpu.get_barrier_semaphore()
    for peer in peers:
        pl.semaphore_signal(barrier, inc=1, device_id=peer, device_id_type=MESH)

    loads = []

    def load(src, dst):
        copy = pltpu.make_async_copy(src, dst, load_sems.at[len(loads)])
        loads.append(copy)
        copy.start()
        return copy

    def columns(half, step):
        return pl.ds(pl.multiple_of((((x + step) % 4) * 2 + half) * 640, 128), 640)

    order = [(turn, step) for turn in range(2) for step in (2, 1, 3, 0)]
    halves = (other, zh)
    cots_load = load(cots_in, cots)
    acts_loads = {}
    for turn, step in order:
        lanes = columns(halves[turn], step)
        acts_loads[turn, step] = load(acts_in.at[:, lanes], acts.at[:, lanes])
    small_loads = [load(pos_in, pos), load(momentum_in, momentum), load(weights_in, weights), load(dct_in, dct)]

    copies = []

    class push:
        def __init__(self, src, dst, target):
            slot = len(copies)
            copies.append(self)
            self.copy = pltpu.make_async_remote_copy(
                src_ref=src, dst_ref=dst, send_sem=send_sems.at[slot], recv_sem=recv_sems.at[slot],
                device_id=target, device_id_type=MESH,
            )
            self.arrived = False
            self.copy.start()

        def wait_recv(self):
            if not self.arrived:
                self.copy.wait_recv()
            self.arrived = True

    def finish():
        for copy in copies:
            copy.wait_recv()
        for copy in copies:
            copy.copy.wait_send()

    place = {2: 0, 1: 1, 3: 2, 0: 3}

    def multiply(c, turn, step):
        if c == 0:
            acts_loads[turn, step].wait()
        out = lax.dot_general(
            acts[:, columns(halves[turn], step)], cots[:, c * WIDE : c * WIDE + WIDE],
            (((0,), (0,)), ((), ())), preferred_element_type=F32,
        ).astype(BF)
        for uy in range(4):
            part[c, 0, turn, place[step], uy] = out[uy * 160 : uy * 160 + 80]
            part[c, 1, turn, uy, place[step]] = out[uy * 160 + 80 : uy * 160 + 160]

    def spot(axis, step):
        return place[step] if axis == 0 else (y + step) % 4

    def add(ref, value):
        ref[...] = (ref[...].astype(F32) + value.astype(F32)).astype(BF)

    class Ring:
        def __init__(self, axis, block, first, up, down):
            self.axis, self.block, self.first, self.up, self.down = axis, block, first, up, down

        def up1(self):
            self.u1 = push(self.block(2, 0), self.first(0), along(self.axis, 1))

        def down1(self):
            self.d1 = push(self.block(2, 1), self.first(1), along(self.axis, -1))

        def up2(self):
            self.u2 = push(self.block(1, 1), self.up(1), along(self.axis, 1))

        def down2(self):
            self.d2 = push(self.block(3, 0), self.down(0), along(self.axis, -1))

        def open(self):
            self.up1()
            self.down1()
            self.up2()
            self.down2()

        def relay(self):
            self.u1.wait_recv()
            add(self.block(1, 0), self.first(0)[...])
            self.u3 = push(self.block(1, 0), self.up(0), along(self.axis, 1))
            self.d1.wait_recv()
            add(self.block(3, 1), self.first(1)[...])
            self.d3 = push(self.block(3, 1), self.down(1), along(self.axis, -1))

        def arrive(self):
            for copy in (self.u2, self.d2, self.u3, self.d3):
                copy.wait_recv()

        def direct(self):
            self.straight = [
                push(self.block(step, h), into(h), along(self.axis, step))
                for step, into in ((2, self.first), (1, self.up), (3, self.down))
                for h in range(2)
            ]

        def arrive_direct(self):
            for copy in self.straight:
                copy.wait_recv()

    def first_ring(c, s, turn):
        return Ring(
            s,
            lambda step, h: part.at[c, s, turn, spot(s, step), pl.ds(2 * h, 2)],
            lambda h: hop.at[c, s, turn, h],
            lambda h: plus.at[c, s, turn, pl.ds(2 * h, 2)],
            lambda h: minus.at[c, s, turn, pl.ds(2 * h, 2)],
        )

    def second_ring(c, s, turn):
        return Ring(
            1 - s,
            lambda step, h: part.at[c, s, turn, spot(s, 0), spot(1 - s, step), :, pl.ds(256 * h, 256)],
            lambda h: hop2.at[c, s, turn, h],
            lambda h: plus2.at[c, s, turn, h],
            lambda h: minus2.at[c, s, turn, h],
        )

    both = range(2)
    firsts = [[[first_ring(c, s, turn) for s in both] for turn in both] for c in both]
    seconds = [[[second_ring(c, s, turn) for s in both] for turn in both] for c in both]

    def close(c, turn):
        for s in both:
            firsts[c][turn][s].arrive()
            ref = part.at[c, s, turn, spot(s, 0)]
            ref[...] = (
                ref[...].astype(F32) + plus[c, s, turn].astype(F32) + minus[c, s, turn].astype(F32)
            ).astype(BF)
            if (c, turn) == (1, 1):
                seconds[c][turn][s].direct()
            else:
                seconds[c][turn][s].open()

    def relay(rings):
        for ring in rings:
            ring.relay()

    def summed(c, s, turn, h):
        value = (
            part[c, s, turn, spot(s, 0), spot(1 - s, 0), :, h * 256 : h * 256 + 256].astype(F32)
            + plus2[c, s, turn, h].astype(F32)
            + minus2[c, s, turn, h].astype(F32)
        )
        return value + hop2[c, s, turn, h].astype(F32) if (c, turn) == (1, 1) else value

    crossing = [[None, None], [None, None]]

    def cross_over(c):
        for s in both:
            seconds[c][0][s].arrive()
            for h in both:
                cross[c, s, :, h * 256 : h * 256 + 256] = summed(c, s, 0, h).astype(BF)
            crossing[c][s] = push(cross.at[c, s], cross_in.at[c, s], device(dz=4))

    sib_copies = [None, None]

    def decode(c):
        for s in both:
            if c == 1:
                seconds[c][1][s].arrive_direct()
            else:
                seconds[c][1][s].arrive()
            crossing[c][s].wait_recv()
            rows = slice(s * 80, s * 80 + 80)
            for h in both:
                cols = slice(c * WIDE + h * 256, c * WIDE + h * 256 + 256)
                grad = summed(c, s, 1, h) + cross_in[c, s, :, h * 256 : h * 256 + 256].astype(F32)
                moment = 0.9 * momentum[rows, cols] + grad
                sparse = dot3(moment, dct[0], dct[1]) * mask[rows, cols]
                decoded = dot3(sparse, dct[2], dct[3])
                new_mom[rows, cols] = moment - decoded
                decoded = decoded.astype(BF)
                sent[c, h, s] = decoded[:, :128]
                sent[c, h, 2 + s] = decoded[:, 128:]
        sib_copies[c] = push(sent.at[c, 1 - core], sib_in.at[c], device(flip=True))

    pair_copies = [[], []]

    def exchange(c):
        sib_copies[c].wait_recv()
        pair[c] = (sent[c, core].astype(F32) + sib_in[c].astype(F32)).astype(BF)
        for d in range(1, 4):
            peer = (zl + d) % 4
            pair_copies[c].append(push(pair.at[c, peer], pair_in.at[c, d - 1], (peer * 2 + core, fsdp)))

    own = 2 * x + zh
    s_me, j_me = zl % 2, zl // 2
    lanes_me = pl.ds(pl.multiple_of(j_me * 128, 128), 128)
    rows_me = pl.ds(pl.multiple_of(s_me * 80, 16), 80)
    spread = [[], []]

    def half_of(c):
        return pl.ds(pl.multiple_of(c * WIDE + core * 256, 256), 256)

    def renew(c):
        for copy in pair_copies[c]:
            copy.wait_recv()
        update = pair[c, zl].astype(F32)
        for d in range(3):
            update = update + pair_in[c, d].astype(F32)
        old = weights[rows_me, pl.ds(pl.multiple_of(c * WIDE + core * 256 + j_me * 128, 128), 128)]
        gathered[c, own, y, s_me, :, lanes_me] = (old.astype(F32) - (0.03 / 8) * update).astype(BF)
        block = gathered.at[c, own, y, s_me, :, lanes_me]
        for d in (4, 3, 5, 2, 6, 1, 7):
            spread[c].append(push(block, block, device(dz=d)))

    near = [[], []]

    def go_near(c):
        for copy in spread[c]:
            copy.wait_recv()
        for s in both:
            block = gathered.at[c, pl.ds(2 * x, 2), y, s]
            near[c].append([push(block, block, along(s, step)) for step in (2, 1, 3)])
        for s in both:
            new_w[s * 80 : s * 80 + 80, half_of(c)] = gathered[c, own, y, s]
            push(gathered.at[c, own, y, s], new_w.at[pl.ds(s * 80, 80), half_of(c)], device(flip=True))

    far = [[], []]

    def go_far(c):
        for s in both:
            for copy in near[c][s]:
                copy.wait_recv()
            block = gathered.at[c, :, y, s] if s == 0 else gathered.at[c, pl.ds(2 * x, 2), :, s]
            far[c].append([push(block, block, along(1 - s, 1)), push(block, block, along(1 - s, -1))])

    def relay_far(c):
        for s in both:
            for copy in far[c][s]:
                copy.wait_recv()
            spots = []
            for h, step in ((0, 3), (1, 1)):
                if s == 0:
                    spots.append(gathered.at[c, pl.ds(4 * h, 4), (y + step) % 4, s])
                else:
                    spots.append(gathered.at[c, 2 * ((x + step) % 4) + h, :, s])
            far[c][s] = [push(spots[0], spots[0], along(1 - s, 1)), push(spots[1], spots[1], along(1 - s, -1))]

    def terms(c, source, step):
        ux = (x + step) % 4
        rows = gathered[c, pl.ds(2 * ux, 2)].reshape(1280, 256)
        return jnp.dot(
            source[:, pl.ds(pl.multiple_of(ux * 1280, 128), 1280)], rows, preferred_element_type=F32
        )

    def deliver(c, k, value):
        if k == 0:
            far_keys[c] = value.astype(BF)
            push(far_keys.at[c], keys.at[:, half_of(c)], device(flip=True))
        else:
            keys[:, half_of(c)] = value.astype(BF)

    sources = ((0, sib_acts), (1, acts))

    def last_product(c):
        for s in both:
            for copy in far[c][s]:
                copy.wait_recv()
        for k, source in sources:
            total[k] = jnp.zeros((512, 256), F32)

            @pl.loop(0, 4)
            def _(step):
                total[k] += terms(c, source, step)

            deliver(c, k, total[k])

    def far_part(c, step):
        block = gathered.at[c, pl.ds(2 * ((x + step) % 4), 2), y, 0]
        return [push(block, block, along(1, 1)), push(block, block, along(1, -1))]

    def relay_part(c, step, copies):
        for copy in copies:
            copy.wait_recv()
        blocks = [gathered.at[c, 2 * ((x + step) % 4) + h, (y + dy) % 4, 0] for h, dy in ((0, 3), (1, 1))]
        return [push(blocks[0], blocks[0], along(1, 1)), push(blocks[1], blocks[1], along(1, -1))]

    cots_load.wait()
    multiply(0, 0, 2)
    pl.semaphore_wait(barrier, len(peers))
    a0, b0 = firsts[0][0]
    a0.up1()
    a0.down1()
    multiply(0, 0, 1)
    a0.up2()
    b0.up1()
    b0.down2()
    multiply(0, 0, 3)
    a0.down2()
    multiply(0, 0, 0)
    b0.down1()
    b0.up2()
    for step in (2, 1, 3, 0):
        multiply(0, 1, step)
    relay(firsts[0][0])
    for ring in firsts[0][1]:
        ring.open()
    for step in (2, 1, 3, 0):
        multiply(1, 0, step)

    acts_copy = push(acts, sib_acts, device(flip=True))
    for copy in small_loads:
        copy.wait()
    places = pos[...].astype(F32).astype(BF)
    lane = lax.broadcasted_iota(jnp.int32, (128, 1024), 1)
    row = lax.broadcasted_iota(jnp.int32, (128, 1024), 0)
    slot = (lax.broadcasted_iota(jnp.int32, (160, 1024), 1) % 64).astype(F32)
    mask[...] = jnp.zeros_like(mask)
    for t in range(8):
        pick = (row == lane // 64 * 8 + t).astype(F32).astype(BF)
        at = lax.dot_general(places, pick, (((0,), (0,)), ((), ())), preferred_element_type=F32)
        mask[...] += (at == slot).astype(F32)

    close(0, 0)
    relay(firsts[0][1])
    for ring in firsts[1][0]:
        ring.up1()
        ring.down1()
    for step in (2, 1, 3, 0):
        multiply(1, 1, step)
    relay(seconds[0][0])
    close(0, 1)
    for ring in firsts[1][0]:
        ring.up2()
        ring.down2()
    cross_over(0)
    relay(seconds[0][1])
    relay(firsts[1][0])
    for ring in firsts[1][1]:
        ring.open()
    decode(0)
    close(1, 0)
    exchange(0)
    relay(firsts[1][1])
    renew(0)
    relay(seconds[1][0])
    close(1, 1)
    cross_over(1)
    go_near(0)
    decode(1)
    go_far(0)
    exchange(1)
    renew(1)
    acts_copy.wait_recv()
    go_near(1)
    relay_far(0)
    for s in both:
        for copy in near[1][s]:
            copy.wait_recv()
    parts = {step: far_part(1, step) for step in (0, 1, 3)}
    block = gathered.at[1, pl.ds(2 * x, 2), :, 1]
    across = [push(block, block, along(0, 1)), push(block, block, along(0, -1))]
    last_product(0)
    parts[0] = relay_part(1, 0, parts[0])
    parts[2] = far_part(1, 2)
    parts[1] = relay_part(1, 1, parts[1])
    parts[3] = relay_part(1, 3, parts[3])
    for copy in across:
        copy.wait_recv()
    blocks = [gathered.at[1, 2 * ((x + dx) % 4) + h, :, 1] for h, dx in ((0, 3), (1, 1))]
    across = [push(blocks[0], blocks[0], along(0, 1)), push(blocks[1], blocks[1], along(0, -1))]
    parts[2] = relay_part(1, 2, parts[2])
    for step in (0, 1, 3, 2):
        for copy in parts[step] + (across if step == 2 else []):
            copy.wait_recv()
        for k, source in sources:
            if step == 0:
                total[k] = terms(1, source, step)
            elif step != 2:
                total[k] += terms(1, source, step)
            else:
                deliver(1, k, total[k] + terms(1, source, step))
    finish()


def hand_over(*refs):
    sources, targets, held, sems = refs[:3], refs[3:6], refs[6:9], refs[9]
    copies = [pltpu.make_async_copy(sources[i], held[i], sems.at[i]) for i in range(3)]
    for copy in copies:
        copy.start()
    out = []
    for i in range(3):
        copies[i].wait()
        out.append(pltpu.make_async_copy(held[i], targets[i], sems.at[3 + i]))
        out[i].start()
    for copy in out:
        copy.wait()


def on_device(activations, cotangents, weights, momentum, positions):
    vmem = pl.BlockSpec(memory_space=pltpu.VMEM)
    anywhere = pl.BlockSpec(memory_space=pl.ANY)
    pos = positions[0].transpose(1, 2, 0).reshape(128, 160)
    dma = pltpu.SemaphoreType.DMA((N_COPIES,))
    shapes = (
        jax.ShapeDtypeStruct((160, 1024), F32),
        jax.ShapeDtypeStruct((160, 1024), BF),
        jax.ShapeDtypeStruct((512, 1024), BF),
    )
    results = pl.pallas_call(
        kernel,
        name="step",
        out_shape=shapes,
        in_specs=[anywhere] * 6,
        out_specs=(vmem, vmem, vmem),
        scratch_shapes=[
            pltpu.VMEM((512, 5120), BF),
            pltpu.VMEM((512, 1024), BF),
            pltpu.VMEM((160, 1024), BF),
            pltpu.VMEM((160, 1024), F32),
            pltpu.VMEM((128, 160), jnp.int32),
            pltpu.VMEM((4, 256, 256), BF),
            pltpu.VMEM((512, 5120), BF),
            pltpu.VMEM((2, 2, 2, 4, 4, 80, WIDE), BF),
            pltpu.VMEM((2, 2, 2, 2, 2, 80, WIDE), BF),
            pltpu.VMEM((2, 2, 2, 4, 80, WIDE), BF),
            pltpu.VMEM((2, 2, 2, 4, 80, WIDE), BF),
            pltpu.VMEM((2, 2, 2, 2, 80, 256), BF),
            pltpu.VMEM((2, 2, 2, 2, 80, 256), BF),
            pltpu.VMEM((2, 2, 2, 2, 80, 256), BF),
            pltpu.VMEM((2, 2, 80, WIDE), BF),
            pltpu.VMEM((2, 2, 80, WIDE), BF),
            pltpu.VMEM((160, 1024), F32),
            pltpu.VMEM((2, 2, 4, 80, 128), BF),
            pltpu.VMEM((2, 4, 80, 128), BF),
            pltpu.VMEM((2, 4, 80, 128), BF),
            pltpu.VMEM((2, 3, 80, 128), BF),
            pltpu.VMEM((2, 8, 4, 2, 80, 256), BF),
            pltpu.VMEM((2, 512, 256), F32),
            pltpu.VMEM((2, 512, 256), BF),
            pltpu.SemaphoreType.DMA((16,)),
            dma,
            dma,
        ],
        compiler_params=pltpu.CompilerParams(
            collective_id=0, has_side_effects=True, vmem_limit_bytes=60 * 2**20
        ),
    )(activations, cotangents, weights, momentum[0], pos, jnp.asarray(transforms()))
    new_mom, new_w, keys = pl.pallas_call(
        hand_over,
        name="hand_over",
        out_shape=shapes,
        in_specs=[anywhere] * 3,
        out_specs=(anywhere,) * 3,
        scratch_shapes=[pltpu.VMEM(shape.shape, shape.dtype) for shape in shapes]
        + [pltpu.SemaphoreType.DMA((6,))],
        compiler_params=pltpu.CompilerParams(vmem_limit_bytes=60 * 2**20),
    )(*results)
    return new_mom[None], new_w, keys


def solution(mesh):
    placed = (
        P(("rep", "fsdp"), None),
        P(("rep", "fsdp"), None),
        P("fsdp", None),
        P("rep", "fsdp", None),
        P("rep", "fsdp", None, None),
    )
    return jax.shard_map(
        on_device,
        mesh=mesh,
        in_specs=placed,
        out_specs=(P("rep", "fsdp", None), P("fsdp", None), P(("rep", "fsdp"), None)),
        check_vma=False,
    )
```

```python
import functools
import math

import jax
import jax.numpy as jnp
import numpy as np
from jax import lax
from jax.experimental import pallas as pl
from jax.experimental.pallas import tpu as pltpu
from jax.sharding import PartitionSpec as P

MESH = pl.DeviceIdType.MESH
BF = jnp.bfloat16
F32 = jnp.float32
N_COPIES = 288
CHUNKS = ((0, 512), (512, 256), (768, 256))
LAST = len(CHUNKS) - 1


def transforms():
    k = np.arange(64, dtype=np.float64)[:, None]
    n = np.arange(64, dtype=np.float64)[None, :]
    table = np.where(k == 0, math.sqrt(1.0 / 64), math.sqrt(2.0 / 64)) * np.cos(math.pi * (2 * n + 1) * k / 128)
    back = np.kron(np.eye(4), table).astype(np.float32)
    high = back.astype(jnp.bfloat16)
    low = (back - high.astype(np.float32)).astype(jnp.bfloat16)
    return np.stack([high.T, low.T, high, low])


def dot3(value, high, low):
    top = value.astype(BF)
    rest = (value - top.astype(F32)).astype(BF)
    dot = functools.partial(jnp.dot, preferred_element_type=F32)
    return dot(top, high) + (dot(rest, high) + dot(top, low))


def kernel(
    acts_in, cots_in, weights_in, momentum_in, pos_in, dct_in,
    new_mom, new_w, keys,
    acts, cots, weights, momentum, pos, dct,
    sib_acts, mask, chunks,
    load_sems, send_sems, recv_sems,
):
    (
        part, hop, plus, minus, hop2, plus2, minus2, cross, cross_in,
        sent, sib_in, pair, pair_in, gathered, total, far_keys,
    ) = zip(*chunks)
    rep, fsdp = lax.axis_index("rep"), lax.axis_index("fsdp")
    x, zh, y = fsdp // 8, (fsdp // 4) % 2, fsdp % 4
    zl, core = rep // 2, rep % 2
    z = zh * 4 + zl
    other = 1 - zh

    def device(dx=0, dy=0, dz=0, flip=False):
        nz = (z + 8 + dz) % 8
        return (
            (nz % 4) * 2 + ((1 - core) if flip else core),
            ((x + 4 + dx) % 4) * 8 + (nz // 4) * 4 + (y + 4 + dy) % 4,
        )

    def along(axis, step):
        return device(dx=step) if axis == 0 else device(dy=step)

    peers = [along(axis, step) for axis in range(2) for step in (1, 2, 3)]
    peers += [device(dz=d) for d in range(1, 8)] + [device(flip=True)]
    loads = []

    def load(src, dst):
        copy = pltpu.make_async_copy(src, dst, load_sems.at[len(loads)])
        loads.append(copy)
        copy.start()
        return copy

    def columns(half, step):
        return pl.ds(pl.multiple_of((((x + step) % 4) * 2 + half) * 640, 128), 640)

    order = [(turn, step) for turn in range(2) for step in (2, 1, 3, 0)]
    halves = (other, zh)
    cots_loads = [load(cots_in.at[:, :512], cots.at[:, :512])]
    acts_loads = {}
    lanes = columns(halves[0], 2)
    acts_loads[0, 2] = load(acts_in.at[:, lanes], acts.at[:, lanes])

    barrier = pltpu.get_barrier_semaphore()
    for peer in peers:
        pl.semaphore_signal(barrier, inc=1, device_id=peer, device_id_type=MESH)

    for turn, step in order[1:]:
        lanes = columns(halves[turn], step)
        acts_loads[turn, step] = load(acts_in.at[:, lanes], acts.at[:, lanes])
    cots_loads.append(load(cots_in.at[:, 512:], cots.at[:, 512:]))
    small_loads = [load(pos_in, pos), load(momentum_in, momentum), load(weights_in, weights), load(dct_in, dct)]

    copies = []

    class push:
        def __init__(self, src, dst, target, when=None, got=None):
            slot = len(copies)
            copies.append(self)
            self.copy = pltpu.make_async_remote_copy(
                src_ref=src, dst_ref=dst, send_sem=send_sems.at[slot], recv_sem=recv_sems.at[slot],
                device_id=target, device_id_type=MESH,
            )
            self.arrived, self.when, self.got = False, when, got
            self.guard(when, self.copy.start)

        def guard(self, condition, act):
            if condition is None:
                act()
            else:
                pl.when(condition)(act)

        def wait_recv(self):
            if not self.arrived:
                self.guard(self.got, self.copy.wait_recv)
            self.arrived = True

        def wait_send(self):
            self.guard(self.when, self.copy.wait_send)

    def finish():
        for copy in copies:
            copy.wait_recv()
        for copy in copies:
            copy.wait_send()

    place = {2: 0, 1: 1, 3: 2, 0: 3}

    def multiply(some, turn, step, at=None):
        first, width = CHUNKS[some[0]][0], sum(CHUNKS[c][1] for c in some)
        out = lax.dot_general(
            acts[:, columns(halves[turn], step)], cots[:, first : first + width],
            (((0,), (0,)), ((), ())), preferred_element_type=F32,
        ).astype(BF)
        at = place[step] if at is None else at
        for c in some:
            cols = slice(CHUNKS[c][0] - first, CHUNKS[c][0] - first + CHUNKS[c][1])
            for uy in range(4):
                part[c][0, turn, at, uy] = out[uy * 160 : uy * 160 + 80, cols]
                part[c][1, turn, uy, at] = out[uy * 160 + 80 : uy * 160 + 160, cols]

    def multiply_all(some, turn):
        @pl.loop(0, 4)
        def _(k):
            multiply(some, turn, (2 - k + 3 * (k // 2) + 2 * (k // 3)) % 4, k)

    def spot(axis, step):
        return place[step] if axis == 0 else (y + step) % 4

    def add(ref, *terms):
        def tile(ref, terms):
            @pl.loop(0, ref.shape[0] // 16)
            def _(k):
                rows = pl.ds(pl.multiple_of(k * 16, 16), 16)
                value = ref[rows].astype(F32)
                for term in terms:
                    value = value + term[rows].astype(F32)
                ref[rows] = value.astype(BF)

        if len(ref.shape) == 2:
            tile(ref, terms)
        else:
            pl.loop(0, ref.shape[0])(lambda i: tile(ref.at[i], [term.at[i] for term in terms]))

    class Ring:
        def __init__(self, axis, block, first, up, down):
            self.axis, self.block, self.first, self.up, self.down = axis, block, first, up, down

        def up1(self):
            self.u1 = push(self.block(2, 0), self.first(0), along(self.axis, 1))

        def down1(self):
            self.d1 = push(self.block(2, 1), self.first(1), along(self.axis, -1))

        def up2(self):
            self.u2 = push(self.block(1, 1), self.up(1), along(self.axis, 1))

        def down2(self):
            self.d2 = push(self.block(3, 0), self.down(0), along(self.axis, -1))

        def open(self):
            self.up1()
            self.down1()
            self.up2()
            self.down2()

        def up3(self):
            self.u1.wait_recv()
            add(self.block(1, 0), self.first(0))
            self.u3 = push(self.block(1, 0), self.up(0), along(self.axis, 1))

        def down3(self):
            self.d1.wait_recv()
            add(self.block(3, 1), self.first(1))
            self.d3 = push(self.block(3, 1), self.down(1), along(self.axis, -1))

        def arrive(self):
            for copy in (self.u2, self.d2, self.u3, self.d3):
                copy.wait_recv()

        def relay(self):
            self.up3()
            self.down3()

    both = range(2)

    def half_cols(c, h):
        half = CHUNKS[c][1] // 2
        return pl.ds(h * half, half)

    def first_ring(c, s, turn):
        return Ring(
            s,
            lambda step, h: part[c].at[s, turn, spot(s, step), pl.ds(2 * h, 2)],
            lambda h: hop[c].at[s, turn, h],
            lambda h: plus[c].at[s, turn, pl.ds(2 * h, 2)],
            lambda h: minus[c].at[s, turn, pl.ds(2 * h, 2)],
        )

    def second_ring(c, s, turn):
        return Ring(
            1 - s,
            lambda step, h: part[c].at[s, turn, spot(s, 0), spot(1 - s, step), :, half_cols(c, h)],
            lambda h: hop2[c].at[s, turn, h],
            lambda h: plus2[c].at[s, turn, h],
            lambda h: minus2[c].at[s, turn, h],
        )

    firsts = [[[first_ring(c, s, turn) for s in both] for turn in both] for c in range(len(CHUNKS))]
    seconds = [[[second_ring(c, s, turn) for s in both] for turn in both] for c in range(len(CHUNKS))]

    def close(c, turn, s):
        firsts[c][turn][s].arrive()
        add(part[c].at[s, turn, spot(s, 0)], plus[c].at[s, turn], minus[c].at[s, turn])
        seconds[c][turn][s].open()

    def summed(c, s, turn, h):
        return (
            part[c][s, turn, spot(s, 0), spot(1 - s, 0), :, half_cols(c, h)].astype(F32)
            + plus2[c][s, turn, h].astype(F32)
            + minus2[c][s, turn, h].astype(F32)
        )

    crossing = [[None, None] for _ in CHUNKS]

    def cross_over(c, s):
        seconds[c][0][s].arrive()
        for h in both:
            cross[c][s, :, half_cols(c, h)] = summed(c, s, 0, h).astype(BF)
        crossing[c][s] = push(cross[c].at[s], cross_in[c].at[s], device(dz=4))

    sib_copies = [None for _ in CHUNKS]

    def decode(c, s):
        seconds[c][1][s].arrive()
        crossing[c][s].wait_recv()
        rows = slice(s * 80, s * 80 + 80)
        for h in both:
            half = CHUNKS[c][1] // 2
            cols = pl.ds(CHUNKS[c][0] + h * half, half)
            grad = summed(c, s, 1, h) + cross_in[c][s, :, half_cols(c, h)].astype(F32)
            moment = 0.9 * momentum[rows, cols] + grad
            table = [dct[i, :half, :half] for i in range(4)]
            sparse = dot3(moment, table[0], table[1]) * mask[rows, cols]
            decoded = dot3(sparse, table[2], table[3])
            new_mom[rows, cols] = moment - decoded
            decoded = decoded.astype(BF)
            for j in range(half // 128):
                sent[c][h, 2 * j + s] = decoded[:, j * 128 : j * 128 + 128]
        if s == 1:
            sib_copies[c] = push(sent[c].at[1 - core], sib_in[c], device(flip=True))

    pair_copies = [[] for _ in CHUNKS]

    def on_duty(c, at):
        return None if CHUNKS[c][1] == 512 else (at + 4) % 4 // 2 == c - 1

    def unit(c, at):
        return at if CHUNKS[c][1] == 512 else at % 2

    def exchange(c):
        sib_copies[c].wait_recv()
        pair[c][...] = (sent[c][core].astype(F32) + sib_in[c][...].astype(F32)).astype(BF)
        for d in range(1, 4):
            peer = (zl + d) % 4
            pair_copies[c].append(
                push(
                    pair[c].at[unit(c, peer)], pair_in[c].at[d - 1], (peer * 2 + core, fsdp),
                    when=on_duty(c, peer), got=on_duty(c, zl),
                )
            )

    own = 2 * x + zh
    s_me, j_me = zl % 2, zl // 2
    rows_me = pl.ds(pl.multiple_of(s_me * 80, 16), 80)
    spread = [[] for _ in CHUNKS]

    def half_of(c):
        first, width = CHUNKS[c]
        return pl.ds(pl.multiple_of(first + core * (width // 2), 128), width // 2)

    def renew(c):
        first, width = CHUNKS[c]
        j = j_me if width == 512 else 0
        lanes_me = pl.ds(pl.multiple_of(j * 128, 128), 128)
        block = gathered[c].at[own, y, s_me, :, lanes_me]
        for copy in pair_copies[c]:
            copy.wait_recv()

        def make():
            update = pair[c][unit(c, zl)].astype(F32)
            for d in range(3):
                update = update + pair_in[c][d].astype(F32)
            old = weights[rows_me, pl.ds(pl.multiple_of(first + core * (width // 2) + j * 128, 128), 128)]
            block[...] = (old.astype(F32) - (0.03 / 8) * update).astype(BF)

        duty = on_duty(c, zl)
        if duty is None:
            make()
        else:
            pl.when(duty)(make)
        for d in (4, 3, 5, 2, 6, 1, 7):
            spread[c].append(push(block, block, device(dz=d), when=duty, got=on_duty(c, zl + 4 - d % 4)))

    near, far, onward = ([[None, None] for _ in CHUNKS] for _ in range(3))

    def go_near(c, s):
        for copy in spread[c]:
            copy.wait_recv()
        block = gathered[c].at[pl.ds(2 * x, 2), y, s]
        near[c][s] = [push(block, block, along(s, step)) for step in (2, 1, 3)]
        new_w[s * 80 : s * 80 + 80, half_of(c)] = gathered[c][own, y, s]
        push(gathered[c].at[own, y, s], new_w.at[pl.ds(s * 80, 80), half_of(c)], device(flip=True))

    def go_far(c, s):
        for copy in near[c][s]:
            copy.wait_recv()
        block = gathered[c].at[:, y, s] if s == 0 else gathered[c].at[pl.ds(2 * x, 2), :, s]
        far[c][s] = [push(block, block, along(1 - s, 1)), push(block, block, along(1 - s, -1))]

    def relay_far(c, s):
        for copy in far[c][s]:
            copy.wait_recv()
        spots = []
        for h, step in ((0, 3), (1, 1)):
            if s == 0:
                spots.append(gathered[c].at[pl.ds(4 * h, 4), (y + step) % 4, s])
            else:
                spots.append(gathered[c].at[2 * ((x + step) % 4) + h, :, s])
        onward[c][s] = [push(spots[0], spots[0], along(1 - s, 1)), push(spots[1], spots[1], along(1 - s, -1))]

    def terms(some, source, step):
        ux = (x + step) % 4
        rows = [gathered[c][pl.ds(2 * ux, 2)].reshape(1280, CHUNKS[c][1] // 2) for c in some]
        rows = jnp.concatenate(rows, axis=1) if len(rows) > 1 else rows[0]
        return jnp.dot(
            source[:, pl.ds(pl.multiple_of(ux * 1280, 128), 1280)], rows, preferred_element_type=F32
        )

    def deliver(c, k, value):
        if k == 0:
            far_keys[c][...] = value.astype(BF)
            push(far_keys[c], keys.at[:, half_of(c)], device(flip=True))
        else:
            keys[:, half_of(c)] = value.astype(BF)

    sources = ((0, sib_acts), (1, acts))

    def last_product(c):
        acts_copy.wait_recv()
        for s in both:
            for copy in onward[c][s]:
                copy.wait_recv()
        for k, source in sources:
            total[c][k] = jnp.zeros(total[c].shape[1:], F32)

            @pl.loop(0, 4)
            def _(step):
                total[c][k] += terms((c,), source, step)

            deliver(c, k, total[c][k])

    def far_part(c, step):
        block = gathered[c].at[pl.ds(2 * ((x + step) % 4), 2), y, 0]
        return [push(block, block, along(1, 1)), push(block, block, along(1, -1))]

    def relay_part(c, step, copies):
        for copy in copies:
            copy.wait_recv()
        blocks = [gathered[c].at[2 * ((x + step) % 4) + h, (y + dy) % 4, 0] for h, dy in ((0, 3), (1, 1))]
        return [push(blocks[0], blocks[0], along(1, 1)), push(blocks[1], blocks[1], along(1, -1))]

    parts, across = {}, []

    def go_last():
        for s in both:
            for copy in near[LAST][s]:
                copy.wait_recv()
        for step in (0, 1, 3):
            parts[step] = far_part(LAST, step)
        block = gathered[LAST].at[pl.ds(2 * x, 2), :, 1]
        across.extend([push(block, block, along(0, 1)), push(block, block, along(0, -1))])

    def relay_last():
        parts[0] = relay_part(LAST, 0, parts[0])
        parts[2] = far_part(LAST, 2)
        parts[1] = relay_part(LAST, 1, parts[1])
        parts[3] = relay_part(LAST, 3, parts[3])
        for copy in across:
            copy.wait_recv()
        blocks = [gathered[LAST].at[2 * ((x + dx) % 4) + h, :, 1] for h, dx in ((0, 3), (1, 1))]
        across.extend([push(blocks[0], blocks[0], along(0, 1)), push(blocks[1], blocks[1], along(0, -1))])
        parts[2] = relay_part(LAST, 2, parts[2])

    cots_loads[0].wait()
    acts_loads[0, 2].wait()
    multiply((0,), 0, 2)
    pl.semaphore_wait(barrier, len(peers))
    a0, b0 = firsts[0][0]
    a0.up1()
    a0.down1()
    acts_loads[0, 1].wait()
    multiply((0,), 0, 1)
    a0.up2()
    b0.up1()
    b0.down2()
    acts_loads[0, 3].wait()
    multiply((0,), 0, 3)
    a0.down2()
    acts_loads[0, 0].wait()
    multiply((0,), 0, 0)
    b0.down1()
    b0.up2()
    for step in (2, 1, 3, 0):
        acts_loads[1, step].wait()
    cots_loads[1].wait()

    multiply_all((0,), 1)
    acts_copy = push(acts, sib_acts, device(flip=True))
    for copy in small_loads:
        copy.wait()
    places = pos[...].astype(F32).astype(BF)
    lane = lax.broadcasted_iota(jnp.int32, (128, 1024), 1)
    row = lax.broadcasted_iota(jnp.int32, (128, 1024), 0)
    slot = (lax.broadcasted_iota(jnp.int32, (160, 1024), 1) % 64).astype(F32)
    mask[...] = jnp.zeros_like(mask)

    @pl.loop(0, 8)
    def _(t):
        pick = (row == lane // 64 * 8 + t).astype(F32).astype(BF)
        at = lax.dot_general(places, pick, (((0,), (0,)), ((), ())), preferred_element_type=F32)
        mask[...] += (at == slot).astype(F32)

    firsts[0][1][0].up1()
    firsts[0][1][0].down1()
    firsts[0][1][1].up1()
    firsts[0][1][1].down1()
    multiply_all((1, 2), 0)
    firsts[0][0][0].up3()
    firsts[0][0][0].down3()
    firsts[0][0][1].up3()
    firsts[0][0][1].down3()
    multiply_all((1, 2), 1)
    firsts[0][1][0].up2()
    firsts[0][1][0].down2()
    firsts[0][1][1].up2()
    firsts[0][1][1].down2()
    firsts[0][1][0].up3()
    firsts[0][1][0].down3()
    firsts[0][1][1].up3()
    firsts[0][1][1].down3()
    close(0, 0, 0)
    close(0, 0, 1)
    firsts[1][0][0].up1()
    firsts[1][0][0].down1()
    firsts[1][0][1].up1()
    firsts[1][0][1].down1()
    firsts[1][0][0].up2()
    firsts[1][0][0].down2()
    firsts[1][0][1].up2()
    firsts[1][0][1].down2()
    close(0, 1, 0)
    close(0, 1, 1)
    seconds[0][0][1].relay()
    seconds[0][0][0].relay()
    firsts[1][0][0].up3()
    firsts[1][0][0].down3()
    firsts[1][0][1].up3()
    firsts[1][0][1].down3()
    firsts[1][1][0].up1()
    firsts[1][1][0].down1()
    firsts[1][1][1].up1()
    firsts[1][1][1].down1()
    seconds[0][1][1].relay()
    seconds[0][1][0].relay()
    cross_over(0, 1)
    firsts[1][1][0].up2()
    firsts[1][1][0].down2()
    firsts[1][1][1].up2()
    cross_over(0, 0)
    firsts[1][1][1].down2()
    firsts[2][0][0].up1()
    close(1, 0, 0)
    close(1, 0, 1)
    firsts[2][0][0].down1()
    firsts[2][0][1].up1()
    firsts[2][0][1].down1()
    firsts[1][1][0].up3()
    firsts[1][1][0].down3()
    firsts[1][1][1].up3()
    firsts[1][1][1].down3()
    firsts[2][0][0].up2()
    firsts[2][0][0].down2()
    firsts[2][0][1].up2()
    firsts[2][0][1].down2()
    seconds[1][0][0].relay()
    firsts[2][1][0].up1()
    firsts[2][0][0].up3()
    firsts[2][1][0].down1()
    seconds[1][0][1].relay()
    firsts[2][1][1].up1()
    firsts[2][1][1].down1()
    firsts[2][0][0].down3()
    firsts[2][0][1].up3()
    decode(0, 0)
    close(1, 1, 0)
    close(1, 1, 1)
    decode(0, 1)
    cross_over(1, 0)
    firsts[2][0][1].down3()
    firsts[2][1][0].up2()
    firsts[2][1][0].down2()
    firsts[2][1][1].up2()
    firsts[2][1][1].down2()
    firsts[2][1][0].up3()
    firsts[2][1][0].down3()
    firsts[2][1][1].up3()
    firsts[2][1][1].down3()
    exchange(0)
    cross_over(1, 1)
    close(2, 0, 0)
    seconds[1][1][1].relay()
    seconds[1][1][0].relay()
    close(2, 0, 1)
    renew(0)
    close(2, 1, 0)
    close(2, 1, 1)
    seconds[2][0][0].relay()
    seconds[2][0][1].relay()
    decode(1, 0)
    decode(1, 1)
    seconds[2][1][0].relay()
    seconds[2][1][1].relay()
    cross_over(2, 0)
    cross_over(2, 1)
    exchange(1)
    go_near(0, 0)
    go_near(0, 1)
    decode(2, 0)
    decode(2, 1)
    renew(1)
    go_far(0, 0)
    go_far(0, 1)
    exchange(2)
    go_near(1, 0)
    go_near(1, 1)
    renew(2)
    relay_far(0, 0)
    relay_far(0, 1)
    go_near(2, 0)
    go_near(2, 1)
    go_far(1, 0)
    go_far(1, 1)
    go_last()
    last_product(0)
    relay_far(1, 0)
    relay_far(1, 1)
    relay_last()

    for s in both:
        for copy in onward[1][s]:
            copy.wait_recv()
    for step in (0, 1, 3, 2):
        for copy in parts[step] + (across if step == 2 else []):
            copy.wait_recv()
        for k, source in sources:
            value = terms((1, 2), source, step)
            if step == 0:
                total[0][k] = value
            elif step != 2:
                total[0][k] += value
            else:
                value = total[0][k] + value
                deliver(1, k, value[:, :128])
                deliver(2, k, value[:, 128:])
    finish()


def hand_over(*refs):
    copies = [pltpu.make_async_copy(refs[i], refs[3 + i], refs[6].at[i]) for i in range(3)]
    for copy in copies:
        copy.start()
    for copy in copies:
        copy.wait()


def chunk_scratch(width):
    half = width // 2
    units = 2 * half // 128
    shapes = [
        (2, 2, 4, 4, 80, width),
        (2, 2, 2, 2, 80, width),
        (2, 2, 4, 80, width),
        (2, 2, 4, 80, width),
        (2, 2, 2, 80, half),
        (2, 2, 2, 80, half),
        (2, 2, 2, 80, half),
        (2, 80, width),
        (2, 80, width),
        (2, units, 80, 128),
        (units, 80, 128),
        (units, 80, 128),
        (3, 80, 128),
        (8, 4, 2, 80, half),
    ]
    held = [pltpu.VMEM(shape, BF) for shape in shapes]
    return (*held, pltpu.VMEM((2, 512, half), F32), pltpu.VMEM((512, half), BF))


def on_device(activations, cotangents, weights, momentum, positions):
    vmem = pl.BlockSpec(memory_space=pltpu.VMEM)
    anywhere = pl.BlockSpec(memory_space=pl.ANY)
    pos = positions[0].transpose(1, 2, 0).reshape(128, 160)
    dma = pltpu.SemaphoreType.DMA((N_COPIES,))
    shapes = (
        jax.ShapeDtypeStruct((160, 1024), F32),
        jax.ShapeDtypeStruct((160, 1024), BF),
        jax.ShapeDtypeStruct((512, 1024), BF),
    )
    results = pl.pallas_call(
        kernel,
        name="step",
        out_shape=tuple(pltpu.VMEM(shape.shape, shape.dtype) for shape in shapes),
        in_specs=[anywhere] * 6,
        out_specs=(vmem, vmem, vmem),
        scratch_shapes=[
            pltpu.VMEM((512, 5120), BF),
            pltpu.VMEM((512, 1024), BF),
            pltpu.VMEM((160, 1024), BF),
            pltpu.VMEM((160, 1024), F32),
            pltpu.VMEM((128, 160), jnp.int32),
            pltpu.VMEM((4, 256, 256), BF),
            pltpu.VMEM((512, 5120), BF),
            pltpu.VMEM((160, 1024), F32),
            [chunk_scratch(width) for first, width in CHUNKS],
            pltpu.SemaphoreType.DMA((16,)),
            dma,
            dma,
        ],
        compiler_params=pltpu.CompilerParams(
            collective_id=0, has_side_effects=True, vmem_limit_bytes=61 * 2**20
        ),
    )(activations, cotangents, weights, momentum[0], pos, jnp.asarray(transforms()))
    new_mom, new_w, keys = pl.pallas_call(
        hand_over,
        name="hand_over",
        out_shape=shapes,
        in_specs=[vmem] * 3,
        out_specs=(anywhere,) * 3,
        scratch_shapes=[pltpu.SemaphoreType.DMA((3,))],
        compiler_params=pltpu.CompilerParams(vmem_limit_bytes=4 * 2**20),
    )(*results)
    return new_mom[None], new_w, keys


def solution(mesh):
    placed = (
        P(("rep", "fsdp"), None),
        P(("rep", "fsdp"), None),
        P("fsdp", None),
        P("rep", "fsdp", None),
        P("rep", "fsdp", None, None),
    )
    return jax.shard_map(
        on_device,
        mesh=mesh,
        in_specs=placed,
        out_specs=(P("rep", "fsdp", None), P("fsdp", None), P(("rep", "fsdp"), None)),
        check_vma=False,
    )
```

```python
import functools
import math

import jax
import jax.numpy as jnp
import numpy as np
from jax import lax
from jax.experimental import pallas as pl
from jax.experimental.pallas import tpu as pltpu
from jax.sharding import PartitionSpec as P

MESH = pl.DeviceIdType.MESH
BF = jnp.bfloat16
F32 = jnp.float32
N_COPIES = 288
CHUNKS = ((0, 512), (512, 256), (768, 256))
LAST = len(CHUNKS) - 1


def transforms():
    k = np.arange(64, dtype=np.float64)[:, None]
    n = np.arange(64, dtype=np.float64)[None, :]
    table = np.where(k == 0, math.sqrt(1.0 / 64), math.sqrt(2.0 / 64)) * np.cos(math.pi * (2 * n + 1) * k / 128)
    back = np.kron(np.eye(4), table).astype(np.float32)
    high = back.astype(jnp.bfloat16)
    low = (back - high.astype(np.float32)).astype(jnp.bfloat16)
    return np.stack([high.T, low.T, high, low])


def dot3(value, high, low):
    top = value.astype(BF)
    rest = (value - top.astype(F32)).astype(BF)
    dot = functools.partial(jnp.dot, preferred_element_type=F32)
    return dot(top, high) + (dot(rest, high) + dot(top, low))


def kernel(
    acts_in, cots_in, weights_in, momentum_in, pos_in, dct_in,
    new_mom, new_w, keys,
    acts, cots, weights, momentum, pos, dct,
    sib_acts, mask, chunks,
    load_sems, send_sems, recv_sems,
):
    (
        part, hop, plus, minus, hop2, plus2, minus2, cross, cross_in,
        sent, pair_in, gathered, total, far_keys,
    ) = zip(*chunks)
    rep, fsdp = lax.axis_index("rep"), lax.axis_index("fsdp")
    x, zh, y = fsdp // 8, (fsdp // 4) % 2, fsdp % 4
    zl, core = rep // 2, rep % 2
    z = zh * 4 + zl
    other = 1 - zh

    def device(dx=0, dy=0, dz=0, flip=False):
        nz = (z + 8 + dz) % 8
        return (
            (nz % 4) * 2 + ((1 - core) if flip else core),
            ((x + 4 + dx) % 4) * 8 + (nz // 4) * 4 + (y + 4 + dy) % 4,
        )

    def along(axis, step):
        return device(dx=step) if axis == 0 else device(dy=step)

    peers = [along(axis, step) for axis in range(2) for step in (1, 2, 3)]
    peers += [device(dz=d) for d in range(1, 8)] + [((zl + d) % 4 * 2 + 1 - core, fsdp) for d in range(4)]
    loads = []

    def load(src, dst):
        copy = pltpu.make_async_copy(src, dst, load_sems.at[len(loads)])
        loads.append(copy)
        copy.start()
        return copy

    def columns(half, step):
        return pl.ds(pl.multiple_of((((x + step) % 4) * 2 + half) * 640, 128), 640)

    order = [(turn, step) for turn in range(2) for step in (2, 1, 3, 0)]
    halves = (other, zh)
    cots_loads = [load(cots_in.at[:, :512], cots.at[:, :512])]
    acts_loads = {}
    lanes = columns(halves[0], 2)
    acts_loads[0, 2] = load(acts_in.at[:, lanes], acts.at[:, lanes])

    barrier = pltpu.get_barrier_semaphore()
    for peer in peers:
        pl.semaphore_signal(barrier, inc=1, device_id=peer, device_id_type=MESH)

    for turn, step in order[1:]:
        lanes = columns(halves[turn], step)
        acts_loads[turn, step] = load(acts_in.at[:, lanes], acts.at[:, lanes])
    cots_loads.append(load(cots_in.at[:, 512:], cots.at[:, 512:]))
    small_loads = [load(pos_in, pos), load(momentum_in, momentum), load(weights_in, weights), load(dct_in, dct)]

    copies = []

    class push:
        def __init__(self, src, dst, target, when=None, got=None):
            slot = len(copies)
            copies.append(self)
            self.copy = pltpu.make_async_remote_copy(
                src_ref=src, dst_ref=dst, send_sem=send_sems.at[slot], recv_sem=recv_sems.at[slot],
                device_id=target, device_id_type=MESH,
            )
            self.arrived, self.when, self.got = False, when, got
            self.guard(when, self.copy.start)

        def guard(self, condition, act):
            if condition is None:
                act()
            else:
                pl.when(condition)(act)

        def wait_recv(self):
            if not self.arrived:
                self.guard(self.got, self.copy.wait_recv)
            self.arrived = True

        def wait_send(self):
            self.guard(self.when, self.copy.wait_send)

    def finish():
        for copy in copies:
            copy.wait_recv()
        for copy in copies:
            copy.wait_send()

    place = {2: 0, 1: 1, 3: 2, 0: 3}

    def multiply(some, turn, step, at=None):
        first, width = CHUNKS[some[0]][0], sum(CHUNKS[c][1] for c in some)
        out = lax.dot_general(
            acts[:, columns(halves[turn], step)], cots[:, first : first + width],
            (((0,), (0,)), ((), ())), preferred_element_type=F32,
        ).astype(BF)
        at = place[step] if at is None else at
        for c in some:
            cols = slice(CHUNKS[c][0] - first, CHUNKS[c][0] - first + CHUNKS[c][1])
            for uy in range(4):
                part[c][0, turn, at, uy] = out[uy * 160 : uy * 160 + 80, cols]
                part[c][1, turn, uy, at] = out[uy * 160 + 80 : uy * 160 + 160, cols]

    def multiply_all(some, turn):
        @pl.loop(0, 4)
        def _(k):
            multiply(some, turn, (2 - k + 3 * (k // 2) + 2 * (k // 3)) % 4, k)

    def spot(axis, step):
        return place[step] if axis == 0 else (y + step) % 4

    def add(ref, *terms):
        def tile(ref, terms):
            @pl.loop(0, ref.shape[0] // 16)
            def _(k):
                rows = pl.ds(pl.multiple_of(k * 16, 16), 16)
                value = ref[rows].astype(F32)
                for term in terms:
                    value = value + term[rows].astype(F32)
                ref[rows] = value.astype(BF)

        if len(ref.shape) == 2:
            tile(ref, terms)
        else:
            pl.loop(0, ref.shape[0])(lambda i: tile(ref.at[i], [term.at[i] for term in terms]))

    class Ring:
        def __init__(self, axis, block, first, up, down):
            self.axis, self.block, self.first, self.up, self.down = axis, block, first, up, down

        def up1(self):
            self.u1 = push(self.block(2, 0), self.first(0), along(self.axis, 1))

        def down1(self):
            self.d1 = push(self.block(2, 1), self.first(1), along(self.axis, -1))

        def up2(self):
            self.u2 = push(self.block(1, 1), self.up(1), along(self.axis, 1))

        def down2(self):
            self.d2 = push(self.block(3, 0), self.down(0), along(self.axis, -1))

        def open(self):
            self.up1()
            self.down1()
            self.up2()
            self.down2()

        def up3(self):
            self.u1.wait_recv()
            add(self.block(1, 0), self.first(0))
            self.u3 = push(self.block(1, 0), self.up(0), along(self.axis, 1))

        def down3(self):
            self.d1.wait_recv()
            add(self.block(3, 1), self.first(1))
            self.d3 = push(self.block(3, 1), self.down(1), along(self.axis, -1))

        def arrive(self):
            for copy in (self.u2, self.d2, self.u3, self.d3):
                copy.wait_recv()

        def relay(self):
            self.up3()
            self.down3()

    both = range(2)

    def half_cols(c, h):
        half = CHUNKS[c][1] // 2
        return pl.ds(h * half, half)

    def first_ring(c, s, turn):
        return Ring(
            s,
            lambda step, h: part[c].at[s, turn, spot(s, step), pl.ds(2 * h, 2)],
            lambda h: hop[c].at[s, turn, h],
            lambda h: plus[c].at[s, turn, pl.ds(2 * h, 2)],
            lambda h: minus[c].at[s, turn, pl.ds(2 * h, 2)],
        )

    def second_ring(c, s, turn):
        return Ring(
            1 - s,
            lambda step, h: part[c].at[s, turn, spot(s, 0), spot(1 - s, step), :, half_cols(c, h)],
            lambda h: hop2[c].at[s, turn, h],
            lambda h: plus2[c].at[s, turn, h],
            lambda h: minus2[c].at[s, turn, h],
        )

    firsts = [[[first_ring(c, s, turn) for s in both] for turn in both] for c in range(len(CHUNKS))]
    seconds = [[[second_ring(c, s, turn) for s in both] for turn in both] for c in range(len(CHUNKS))]

    def close(c, turn, s):
        firsts[c][turn][s].arrive()
        add(part[c].at[s, turn, spot(s, 0)], plus[c].at[s, turn], minus[c].at[s, turn])
        seconds[c][turn][s].open()

    def summed(c, s, turn, h):
        return (
            part[c][s, turn, spot(s, 0), spot(1 - s, 0), :, half_cols(c, h)].astype(F32)
            + plus2[c][s, turn, h].astype(F32)
            + minus2[c][s, turn, h].astype(F32)
        )

    crossing = [[None, None] for _ in CHUNKS]

    def cross_over(c, s):
        seconds[c][0][s].arrive()
        for h in both:
            cross[c][s, :, half_cols(c, h)] = summed(c, s, 0, h).astype(BF)
        crossing[c][s] = push(cross[c].at[s], cross_in[c].at[s], device(dz=4))

    def decode(c, s):
        seconds[c][1][s].arrive()
        crossing[c][s].wait_recv()
        rows = slice(s * 80, s * 80 + 80)
        for h in both:
            half = CHUNKS[c][1] // 2
            cols = pl.ds(CHUNKS[c][0] + h * half, half)
            grad = summed(c, s, 1, h) + cross_in[c][s, :, half_cols(c, h)].astype(F32)
            moment = 0.9 * momentum[rows, cols] + grad
            table = [dct[i, :half, :half] for i in range(4)]
            sparse = dot3(moment, table[0], table[1]) * mask[rows, cols]
            decoded = dot3(sparse, table[2], table[3])
            new_mom[rows, cols] = moment - decoded
            decoded = decoded.astype(BF)
            for j in range(half // 128):
                sent[c][h, 2 * j + s] = decoded[:, j * 128 : j * 128 + 128]
        if s == 1:
            exchange(c)

    pair_copies = [[] for _ in CHUNKS]

    def on_duty(c, at):
        return None if CHUNKS[c][1] == 512 else (at + 4) % 4 // 2 == c - 1

    def unit(c, at):
        return at if CHUNKS[c][1] == 512 else at % 2

    def exchange(c):
        for d in range(4):
            peer = (zl + d) % 4
            for flip in range(2):
                if d + flip > 0:
                    side = (1 - core) if flip else core
                    pair_copies[c].append(
                        push(
                            sent[c].at[side, unit(c, peer)], pair_in[c].at[2 * d + flip - 1],
                            (peer * 2 + side, fsdp), when=on_duty(c, peer), got=on_duty(c, zl),
                        )
                    )

    own = 2 * x + zh
    s_me, j_me = zl % 2, zl // 2
    rows_me = pl.ds(pl.multiple_of(s_me * 80, 16), 80)
    spread = [[] for _ in CHUNKS]

    def half_of(c):
        first, width = CHUNKS[c]
        return pl.ds(pl.multiple_of(first + core * (width // 2), 128), width // 2)

    def renew(c):
        first, width = CHUNKS[c]
        j = j_me if width == 512 else 0
        lanes_me = pl.ds(pl.multiple_of(j * 128, 128), 128)
        block = gathered[c].at[own, y, s_me, :, lanes_me]
        for copy in pair_copies[c]:
            copy.wait_recv()

        def make():
            update = sent[c][core, unit(c, zl)].astype(F32)
            for d in range(7):
                update = update + pair_in[c][d].astype(F32)
            old = weights[rows_me, pl.ds(pl.multiple_of(first + core * (width // 2) + j * 128, 128), 128)]
            block[...] = (old.astype(F32) - (0.03 / 8) * update).astype(BF)

        duty = on_duty(c, zl)
        if duty is None:
            make()
        else:
            pl.when(duty)(make)
        for d in (4, 3, 5, 2, 6, 1, 7):
            spread[c].append(push(block, block, device(dz=d), when=duty, got=on_duty(c, zl + 4 - d % 4)))

    near, far, onward = ([[None, None] for _ in CHUNKS] for _ in range(3))

    def go_near(c, s):
        for copy in spread[c]:
            copy.wait_recv()
        block = gathered[c].at[pl.ds(2 * x, 2), y, s]
        near[c][s] = [push(block, block, along(s, step)) for step in (2, 1, 3)]
        new_w[s * 80 : s * 80 + 80, half_of(c)] = gathered[c][own, y, s]
        push(gathered[c].at[own, y, s], new_w.at[pl.ds(s * 80, 80), half_of(c)], device(flip=True))

    def go_far(c, s):
        for copy in near[c][s]:
            copy.wait_recv()
        block = gathered[c].at[:, y, s] if s == 0 else gathered[c].at[pl.ds(2 * x, 2), :, s]
        far[c][s] = [push(block, block, along(1 - s, 1)), push(block, block, along(1 - s, -1))]

    def relay_far(c, s):
        for copy in far[c][s]:
            copy.wait_recv()
        spots = []
        for h, step in ((0, 3), (1, 1)):
            if s == 0:
                spots.append(gathered[c].at[pl.ds(4 * h, 4), (y + step) % 4, s])
            else:
                spots.append(gathered[c].at[2 * ((x + step) % 4) + h, :, s])
        onward[c][s] = [push(spots[0], spots[0], along(1 - s, 1)), push(spots[1], spots[1], along(1 - s, -1))]

    def terms(some, source, step):
        ux = (x + step) % 4
        rows = [gathered[c][pl.ds(2 * ux, 2)].reshape(1280, CHUNKS[c][1] // 2) for c in some]
        rows = jnp.concatenate(rows, axis=1) if len(rows) > 1 else rows[0]
        return jnp.dot(
            source[:, pl.ds(pl.multiple_of(ux * 1280, 128), 1280)], rows, preferred_element_type=F32
        )

    def deliver(c, k, value):
        if k == 0:
            far_keys[c][...] = value.astype(BF)
            push(far_keys[c], keys.at[:, half_of(c)], device(flip=True))
        else:
            keys[:, half_of(c)] = value.astype(BF)

    sources = ((0, sib_acts), (1, acts))

    def last_product(c):
        acts_copy.wait_recv()
        for s in both:
            for copy in onward[c][s]:
                copy.wait_recv()
        for k, source in sources:
            total[c][k] = jnp.zeros(total[c].shape[1:], F32)

            @pl.loop(0, 4)
            def _(step):
                total[c][k] += terms((c,), source, step)

            deliver(c, k, total[c][k])

    def far_part(c, step):
        block = gathered[c].at[pl.ds(2 * ((x + step) % 4), 2), y, 0]
        return [push(block, block, along(1, 1)), push(block, block, along(1, -1))]

    def relay_part(c, step, copies):
        for copy in copies:
            copy.wait_recv()
        blocks = [gathered[c].at[2 * ((x + step) % 4) + h, (y + dy) % 4, 0] for h, dy in ((0, 3), (1, 1))]
        return [push(blocks[0], blocks[0], along(1, 1)), push(blocks[1], blocks[1], along(1, -1))]

    parts, across = {}, []

    def go_last():
        for s in both:
            for copy in near[LAST][s]:
                copy.wait_recv()
        for step in (0, 1, 3):
            parts[step] = far_part(LAST, step)
        block = gathered[LAST].at[pl.ds(2 * x, 2), :, 1]
        across.extend([push(block, block, along(0, 1)), push(block, block, along(0, -1))])

    def relay_last():
        parts[0] = relay_part(LAST, 0, parts[0])
        parts[2] = far_part(LAST, 2)
        parts[1] = relay_part(LAST, 1, parts[1])
        parts[3] = relay_part(LAST, 3, parts[3])
        for copy in across:
            copy.wait_recv()
        blocks = [gathered[LAST].at[2 * ((x + dx) % 4) + h, :, 1] for h, dx in ((0, 3), (1, 1))]
        across.extend([push(blocks[0], blocks[0], along(0, 1)), push(blocks[1], blocks[1], along(0, -1))])
        parts[2] = relay_part(LAST, 2, parts[2])

    cots_loads[0].wait()
    acts_loads[0, 2].wait()
    multiply((0,), 0, 2)
    pl.semaphore_wait(barrier, len(peers))
    a0, b0 = firsts[0][0]
    a0.up1()
    a0.down1()
    acts_loads[0, 1].wait()
    multiply((0,), 0, 1)
    a0.up2()
    b0.up1()
    b0.down2()
    acts_loads[0, 3].wait()
    multiply((0,), 0, 3)
    a0.down2()
    acts_loads[0, 0].wait()
    multiply((0,), 0, 0)
    b0.down1()
    b0.up2()
    for step in (2, 1, 3, 0):
        acts_loads[1, step].wait()
    cots_loads[1].wait()

    multiply_all((0,), 1)
    acts_copy = push(acts, sib_acts, device(flip=True))
    for copy in small_loads:
        copy.wait()
    places = pos[...].astype(F32).astype(BF)
    lane = lax.broadcasted_iota(jnp.int32, (128, 1024), 1)
    row = lax.broadcasted_iota(jnp.int32, (128, 1024), 0)
    slot = (lax.broadcasted_iota(jnp.int32, (160, 1024), 1) % 64).astype(F32)
    mask[...] = jnp.zeros_like(mask)

    @pl.loop(0, 8)
    def _(t):
        pick = (row == lane // 64 * 8 + t).astype(F32).astype(BF)
        at = lax.dot_general(places, pick, (((0,), (0,)), ((), ())), preferred_element_type=F32)
        mask[...] += (at == slot).astype(F32)

    firsts[0][1][0].up1()
    firsts[0][1][0].down1()
    firsts[0][1][1].up1()
    firsts[0][1][1].down1()
    multiply_all((1, 2), 0)
    firsts[0][0][0].up3()
    firsts[0][0][0].down3()
    firsts[0][0][1].up3()
    firsts[0][0][1].down3()
    multiply_all((1, 2), 1)
    firsts[0][1][0].up2()
    firsts[0][1][0].down2()
    firsts[0][1][1].up2()
    firsts[0][1][1].down2()
    firsts[0][1][0].up3()
    firsts[0][1][0].down3()
    firsts[0][1][1].up3()
    firsts[0][1][1].down3()
    close(0, 0, 0)
    close(0, 0, 1)
    firsts[1][0][0].up1()
    firsts[1][0][0].down1()
    firsts[1][0][1].up1()
    firsts[1][0][1].down1()
    firsts[1][0][0].up2()
    firsts[1][0][0].down2()
    firsts[1][0][1].up2()
    firsts[1][0][1].down2()
    close(0, 1, 0)
    close(0, 1, 1)
    seconds[0][0][1].relay()
    seconds[0][0][0].relay()
    firsts[1][0][0].up3()
    firsts[1][0][0].down3()
    firsts[1][0][1].up3()
    firsts[1][0][1].down3()
    firsts[1][1][0].up1()
    firsts[1][1][0].down1()
    firsts[1][1][1].up1()
    firsts[1][1][1].down1()
    seconds[0][1][1].relay()
    seconds[0][1][0].relay()
    cross_over(0, 1)
    firsts[1][1][0].up2()
    firsts[1][1][0].down2()
    firsts[1][1][1].up2()
    cross_over(0, 0)
    firsts[1][1][1].down2()
    firsts[2][0][0].up1()
    close(1, 0, 0)
    close(1, 0, 1)
    firsts[2][0][0].down1()
    firsts[2][0][1].up1()
    firsts[2][0][1].down1()
    firsts[1][1][0].up3()
    firsts[1][1][0].down3()
    firsts[1][1][1].up3()
    firsts[1][1][1].down3()
    firsts[2][0][0].up2()
    firsts[2][0][0].down2()
    firsts[2][0][1].up2()
    firsts[2][0][1].down2()
    seconds[1][0][0].relay()
    firsts[2][1][0].up1()
    firsts[2][0][0].up3()
    firsts[2][1][0].down1()
    seconds[1][0][1].relay()
    firsts[2][1][1].up1()
    firsts[2][1][1].down1()
    firsts[2][0][0].down3()
    firsts[2][0][1].up3()
    decode(0, 0)
    close(1, 1, 0)
    close(1, 1, 1)
    decode(0, 1)
    cross_over(1, 0)
    firsts[2][0][1].down3()
    firsts[2][1][0].up2()
    firsts[2][1][0].down2()
    firsts[2][1][1].up2()
    firsts[2][1][1].down2()
    firsts[2][1][0].up3()
    firsts[2][1][0].down3()
    firsts[2][1][1].up3()
    firsts[2][1][1].down3()
    cross_over(1, 1)
    close(2, 0, 0)
    seconds[1][1][1].relay()
    seconds[1][1][0].relay()
    close(2, 0, 1)
    renew(0)
    close(2, 1, 0)
    close(2, 1, 1)
    seconds[2][0][0].relay()
    seconds[2][0][1].relay()
    decode(1, 0)
    decode(1, 1)
    seconds[2][1][0].relay()
    seconds[2][1][1].relay()
    cross_over(2, 0)
    cross_over(2, 1)
    go_near(0, 0)
    go_near(0, 1)
    decode(2, 0)
    decode(2, 1)
    renew(1)
    go_far(0, 0)
    go_far(0, 1)
    go_near(1, 0)
    go_near(1, 1)
    renew(2)
    relay_far(0, 0)
    relay_far(0, 1)
    go_near(2, 0)
    go_near(2, 1)
    go_far(1, 0)
    go_far(1, 1)
    go_last()
    last_product(0)
    relay_far(1, 0)
    relay_far(1, 1)
    relay_last()

    for s in both:
        for copy in onward[1][s]:
            copy.wait_recv()
    for step in (0, 1, 3, 2):
        for copy in parts[step] + (across if step == 2 else []):
            copy.wait_recv()
        for k, source in sources:
            value = terms((1, 2), source, step)
            if step == 0:
                total[0][k] = value
            elif step != 2:
                total[0][k] += value
            else:
                value = total[0][k] + value
                deliver(1, k, value[:, :128])
                deliver(2, k, value[:, 128:])
    finish()


def hand_over(*refs):
    copies = [pltpu.make_async_copy(refs[i], refs[3 + i], refs[6].at[i]) for i in range(3)]
    for copy in copies:
        copy.start()
    for copy in copies:
        copy.wait()


def chunk_scratch(width):
    half = width // 2
    units = 2 * half // 128
    shapes = [
        (2, 2, 4, 4, 80, width),
        (2, 2, 2, 2, 80, width),
        (2, 2, 4, 80, width),
        (2, 2, 4, 80, width),
        (2, 2, 2, 80, half),
        (2, 2, 2, 80, half),
        (2, 2, 2, 80, half),
        (2, 80, width),
        (2, 80, width),
        (2, units, 80, 128),
        (7, 80, 128),
        (8, 4, 2, 80, half),
    ]
    held = [pltpu.VMEM(shape, BF) for shape in shapes]
    return (*held, pltpu.VMEM((2, 512, half), F32), pltpu.VMEM((512, half), BF))


def on_device(activations, cotangents, weights, momentum, positions):
    vmem = pl.BlockSpec(memory_space=pltpu.VMEM)
    anywhere = pl.BlockSpec(memory_space=pl.ANY)
    pos = positions[0].transpose(1, 2, 0).reshape(128, 160)
    dma = pltpu.SemaphoreType.DMA((N_COPIES,))
    shapes = (
        jax.ShapeDtypeStruct((160, 1024), F32),
        jax.ShapeDtypeStruct((160, 1024), BF),
        jax.ShapeDtypeStruct((512, 1024), BF),
    )
    results = pl.pallas_call(
        kernel,
        name="step",
        out_shape=tuple(pltpu.VMEM(shape.shape, shape.dtype) for shape in shapes),
        in_specs=[anywhere] * 6,
        out_specs=(vmem, vmem, vmem),
        scratch_shapes=[
            pltpu.VMEM((512, 5120), BF),
            pltpu.VMEM((512, 1024), BF),
            pltpu.VMEM((160, 1024), BF),
            pltpu.VMEM((160, 1024), F32),
            pltpu.VMEM((128, 160), jnp.int32),
            pltpu.VMEM((4, 256, 256), BF),
            pltpu.VMEM((512, 5120), BF),
            pltpu.VMEM((160, 1024), F32),
            [chunk_scratch(width) for first, width in CHUNKS],
            pltpu.SemaphoreType.DMA((16,)),
            dma,
            dma,
        ],
        compiler_params=pltpu.CompilerParams(
            collective_id=0, has_side_effects=True, vmem_limit_bytes=61 * 2**20
        ),
    )(activations, cotangents, weights, momentum[0], pos, jnp.asarray(transforms()))
    new_mom, new_w, keys = pl.pallas_call(
        hand_over,
        name="hand_over",
        out_shape=shapes,
        in_specs=[vmem] * 3,
        out_specs=(anywhere,) * 3,
        scratch_shapes=[pltpu.SemaphoreType.DMA((3,))],
        compiler_params=pltpu.CompilerParams(vmem_limit_bytes=4 * 2**20),
    )(*results)
    return new_mom[None], new_w, keys


def solution(mesh):
    placed = (
        P(("rep", "fsdp"), None),
        P(("rep", "fsdp"), None),
        P("fsdp", None),
        P("rep", "fsdp", None),
        P("rep", "fsdp", None, None),
    )
    return jax.shard_map(
        on_device,
        mesh=mesh,
        in_specs=placed,
        out_specs=(P("rep", "fsdp", None), P("fsdp", None), P(("rep", "fsdp"), None)),
        check_vma=False,
    )
```
